256 devices in a mesh: dp: 16 (over z_hi, y, core), mp: 16 (over x, z_lo).
Axes of the slice: x: 4, y: 4, z: 8 (z_hi: 2, z_lo: 4; z = z_hi * 4 + z_lo), core: 2. Of those that a mesh axis runs over, the one named last changes fastest.
Arguments:
- student_rows: bfloat16 [12288, 256], P('dp'), may hold values from -12 to 12
- teacher_rows: bfloat16 [12288, 256], P('dp'), may hold values from -12 to 12
- student_protos: bfloat16 [256, 131072], P(None, 'mp'), may hold values from -12 to 12
- teacher_protos: bfloat16 [256, 131072], P(None, 'mp'), may hold values from -12 to 12
- center: float32 [131072], P('mp'), may hold values from -0.25 to 0.25
- row_weight: float32 [12288], P('dp'), may hold values from 0.25 to 4
Outputs:
- grad_rows: float32 [12288, 256], P('dp')
- proto_grad: float32 [256, 131072], P('dp', 'mp')
The draws below stay inside these ranges and needn't reach their ends.
All inputs are finite; a program needn't handle non-finite values.
Results may differ from the reference program's by a relative error of at most 0.012.
The reference program's roundings to bfloat16 on the way (of `z_student`, `z_teacher`, `w_student`, `w_teacher` and `grad_logit`) count: a program that leaves them out, or rounds other values in their place, can miss the bound.
Values sent between devices are 32-bit elements; how exact they have to be, the bound alone decides.
No kernel may reach another device: no remote copies, remote signals or barrier semaphores. Data moves between devices by JAX's collectives and lax.ppermute only.
A program may use at most 192 MiB of HBM per device.

```python
import math
import jax
import jax.numpy as jnp
from jax import lax

B = 256
K = 131072
ROWS = 12288


def feature_scales(key):
    low = math.log(0.05)
    high = math.log(2.0)
    return jnp.exp(jax.random.uniform(jax.random.fold_in(key, 11), (B,), jnp.float32, low, high))


def base_values(key, shape):
    return jax.random.normal(key, shape, jnp.float32)


def row_base(key):
    values = base_values(jax.random.fold_in(key, 23), (ROWS, B))
    return values


def proto_base(key):
    return base_values(jax.random.fold_in(key, 31), (B, K))


def draw_student_rows(key, part):
    values = row_base(key) * feature_scales(key)[None, :]
    return jnp.clip(values, -12.0, 12.0).astype(jnp.bfloat16)


def draw_teacher_rows(key, part):
    noise = jax.random.normal(jax.random.fold_in(key, 29), (ROWS, B), jnp.float32)
    values = (row_base(key) + 0.6 * noise) * feature_scales(key)[None, :]
    return jnp.clip(values, -12.0, 12.0).astype(jnp.bfloat16)


def draw_student_protos(key, part):
    values = proto_base(key) * feature_scales(key)[:, None]
    return jnp.clip(values, -12.0, 12.0).astype(jnp.bfloat16)


def draw_teacher_protos(key, part):
    noise = jax.random.normal(jax.random.fold_in(key, 37), (B, K), jnp.float32)
    values = (proto_base(key) + 0.3 * noise) * feature_scales(key)[:, None]
    return jnp.clip(values, -12.0, 12.0).astype(jnp.bfloat16)


def steps_of(rng, dims, pieces, low, high):
    loudness = 1.0
    for position, shards_of in pieces:
        steps = jax.random.uniform(jax.random.fold_in(jax.random.fold_in(rng, 6), position), (shards_of,), jnp.float32, low / len(pieces), high / len(pieces))
        loudness = loudness * jnp.repeat(jnp.exp(steps), dims[position] // shards_of).reshape((-1,) + (1,) * (len(dims) - 1 - position))
    return loudness


def scatter_about(own_key, dims, scale, reach, cuts=(), kind=jnp.bfloat16):
    entries = jax.random.normal(own_key, dims, jnp.float32) * scale
    if len(cuts) > 0:
        entries = steps_of(own_key, dims, cuts, -0.22, 0.18) * entries
    return jnp.clip(entries, min=-reach, max=reach).astype(kind)


def setup_inputs(seed: int = 0) -> dict:
    splits = jax.random.split(jax.random.key(seed), 7)
    student_rows = draw_student_rows(jax.random.fold_in(splits[6], 71), 0)
    teacher_rows = draw_teacher_rows(jax.random.fold_in(splits[6], 71), 0)
    student_protos = draw_student_protos(jax.random.fold_in(splits[6], 71), 0)
    teacher_protos = draw_teacher_protos(jax.random.fold_in(splits[6], 71), 0)
    center = scatter_about(splits[4], (K,), 0.05, 0.25, ((0, 16),), jnp.float32)
    row_weight = jnp.clip(jnp.exp(math.log(4.0) - 2.7725887 * jax.random.uniform(splits[5], (ROWS,), jnp.float32) ** steps_of(splits[5], (ROWS,), ((0, 16),), -0.2, 0.2)), 0.25, 4.0)
    return {"student_rows": student_rows, "teacher_rows": teacher_rows, "student_protos": student_protos, "teacher_protos": teacher_protos, "center": center, "row_weight": row_weight}


student_temp = 0.1
teacher_temp = 0.04
norm_eps = 1e-06

def reference(student_rows, teacher_rows, student_protos, teacher_protos, center, row_weight):
    s_full = student_rows.astype(jnp.float32)
    row_norm = jnp.sqrt(lax.optimization_barrier(jnp.sum(s_full * s_full, axis=1, keepdims=True)) + norm_eps)
    z_unit = s_full / row_norm
    z_student = z_unit.astype(jnp.bfloat16)
    t_full = teacher_rows.astype(jnp.float32)
    z_teacher = (t_full / jnp.sqrt(lax.optimization_barrier(jnp.sum(t_full * t_full, axis=1, keepdims=True)) + norm_eps)).astype(jnp.bfloat16)
    v_full = student_protos.astype(jnp.float32)
    col_norm = jnp.sqrt(lax.optimization_barrier(jnp.sum(v_full * v_full, axis=0, keepdims=True)) + norm_eps)
    w_student = (v_full / col_norm).astype(jnp.bfloat16)
    u_full = teacher_protos.astype(jnp.float32)
    w_teacher = (u_full / jnp.sqrt(lax.optimization_barrier(jnp.sum(u_full * u_full, axis=0, keepdims=True)) + norm_eps)).astype(jnp.bfloat16)
    total_rows = student_rows.shape[0]
    block = math.gcd(total_rows, 512)
    blocks = total_rows // block

    def one_block(grad_w, index):
        start = (index * block).astype(jnp.int32)
        zs_block = lax.dynamic_slice_in_dim(z_student, start, block, 0)
        zt_block = lax.dynamic_slice_in_dim(z_teacher, start, block, 0)
        weights = lax.dynamic_slice_in_dim(row_weight, start, block, 0)
        s_logit = jnp.dot(zs_block, w_student, preferred_element_type=jnp.float32)
        t_logit = jnp.dot(zt_block, w_teacher, preferred_element_type=jnp.float32)
        e_student = jnp.exp((s_logit - 1.0) / student_temp)
        e_teacher = jnp.exp((t_logit - center[None, :] - 1.0) / teacher_temp)
        sum_student = lax.optimization_barrier(jnp.sum(e_student, axis=1, keepdims=True))
        sum_teacher = lax.optimization_barrier(jnp.sum(e_teacher, axis=1, keepdims=True))
        grad_logit = (weights[:, None] * (e_student / sum_student - e_teacher / sum_teacher) / student_temp).astype(jnp.bfloat16)
        grad_unit = jnp.dot(grad_logit, w_student.T, preferred_element_type=jnp.float32)
        grad_w = grad_w + jnp.dot(zs_block.T, grad_logit, preferred_element_type=jnp.float32)
        return (grad_w, grad_unit)
    grad_w, stacked = lax.scan(one_block, jnp.zeros(student_protos.shape, jnp.float32), jnp.arange(blocks, dtype=jnp.int32))
    grad_unit = stacked.reshape(total_rows, student_rows.shape[1])
    grad_rows = (grad_unit - z_unit * lax.optimization_barrier(jnp.sum(z_unit * grad_unit, axis=1, keepdims=True))) / row_norm
    w_float = w_student.astype(jnp.float32)
    col_dot = lax.optimization_barrier(jnp.sum(w_float * grad_w, axis=0, keepdims=True))
    proto_grad = (grad_w - w_float * col_dot) / col_norm
    return (grad_rows, proto_grad)
```

```python
import functools
import jax
import jax.numpy as jnp
import numpy as np
from jax import lax
from jax.experimental import pallas as pl
from jax.experimental.pallas import tpu as pltpu
from jax.sharding import PartitionSpec as P

student_temp = 0.1
teacher_temp = 0.04
norm_eps = 1e-06
LOG2E = 1.4426950408889634
F32 = jnp.float32
BF16 = jnp.bfloat16
TILE = 512
ROWBLK = 256
CHUNKS = (1024, 1536, 1536)
MIB = 1 << 20


def call(kernel, out, *args, vmem=40, flops=0, nbytes=0, **kw):
    return pl.pallas_call(
        kernel,
        out_shape=out,
        compiler_params=pltpu.CompilerParams(vmem_limit_bytes=vmem * MIB),
        cost_estimate=pl.CostEstimate(flops=flops, bytes_accessed=nbytes, transcendentals=0),
        **kw,
    )(*args)


def shape(dims, dtype=F32):
    return jax.ShapeDtypeStruct(dims, dtype)


def prep_kernel(s_ref, t_ref, z_ref):
    for i, ref in enumerate((s_ref, t_ref)):
        v = ref[...].astype(F32)
        z_ref[i] = v / jnp.sqrt(jnp.sum(v * v, axis=1, keepdims=True) + norm_eps)


def unit_columns(ref):
    v = ref[...].astype(F32)
    inv = 1.0 / jnp.sqrt(jnp.sum(v * v, axis=0, keepdims=True) + norm_eps)
    return (v * inv).astype(BF16), inv


def logits_pass(z_ref, w_s, w_t, center_ref, es_ref, et_ref, sums_ref, zb, acc, last):
    @pl.when(pl.program_id(0) == 0)
    def _():
        zb[...] = z_ref[...].astype(BF16)
        acc[...] = jnp.zeros_like(acc)

    shift = center_ref[...] * (LOG2E / teacher_temp)
    rows = zb.shape[1]
    for r in range(rows // ROWBLK):
        part = pl.ds(r * ROWBLK, ROWBLK)
        for i, (w, e_ref) in enumerate(((w_s, es_ref), (w_t, et_ref))):
            logit = jnp.dot(zb[i, part, :], w, preferred_element_type=F32)
            if i == 0:
                e = jnp.exp2(logit * (LOG2E / student_temp))
            else:
                e = jnp.exp2(logit * (LOG2E / teacher_temp) - shift)
            total = e[:, :128]
            for k in range(1, TILE // 128):
                total = total + e[:, k * 128 : (k + 1) * 128]
            acc[i, part, :] += total
            e_ref[part, :] = e.astype(BF16)

    @pl.when(pl.program_id(0) == last)
    def _():
        for i in range(2):
            sums_ref[i : i + 1, :] = jnp.sum(acc[i].T, axis=0, keepdims=True)


def own_kernel(last, core_ref, z_ref, sp_ref, tp_ref, center_ref,
               es_ref, et_ref, ws_ref, wt_ref, inv_ref, sums_ref, zb, acc):
    w_s, inv = unit_columns(sp_ref)
    w_t, _ = unit_columns(tp_ref)
    ws_ref[...] = w_s
    wt_ref[...] = w_t
    inv_ref[...] = inv
    logits_pass(z_ref, w_s, w_t, center_ref, es_ref, et_ref, sums_ref, zb, acc, last)


def other_kernel(last, core_ref, z_ref, ws_ref, wt_ref, center_ref, mine_ref, weight_ref,
                 es_ref, et_ref, pay_ref, zb, acc):
    logits_pass(z_ref, ws_ref[...], wt_ref[...], center_ref, es_ref, et_ref,
                pay_ref.at[2:4], zb, acc, last)

    @pl.when(pl.program_id(0) == 0)
    def _():
        pay_ref[0:2, :] = mine_ref[...]
        pay_ref[4:5, :] = weight_ref[...]
        pay_ref[5:8, :] = jnp.zeros_like(pay_ref[5:8, :])


def chip_kernel(mine_ref, theirs_ref, out_ref):
    out_ref[0:2, :] = mine_ref[0:2, :] + theirs_ref[2:4, :]
    out_ref[2:4, :] = mine_ref[2:4, :] + theirs_ref[0:2, :]
    out_ref[4:5, :] = mine_ref[4:5, :]
    out_ref[5:6, :] = theirs_ref[4:5, :]
    out_ref[6:8, :] = jnp.zeros_like(out_ref[6:8, :])


def add4_kernel(a_ref, b_ref, c_ref, d_ref, out_ref):
    out_ref[0:4, :] = a_ref[0:4, :] + b_ref[0:4, :] + c_ref[0:4, :] + d_ref[0:4, :]
    out_ref[4:8, :] = a_ref[4:8, :]


def factors_kernel(a_ref, b_ref, c_ref, d_ref, out_ref):
    total = a_ref[0:4, :] + b_ref[0:4, :] + c_ref[0:4, :] + d_ref[0:4, :]
    for i in range(4):
        weight = a_ref[4 + i // 2 : 5 + i // 2, :]
        f = weight / (total[i : i + 1, :] * student_temp)
        out_ref[i] = jnp.broadcast_to(f, (128, f.shape[1])).T


def unit_kernel(es_ref, et_ref, ws_ref, z_ref, perm_ref, u_ref, zt_ref):
    @pl.when(pl.program_id(0) == 0)
    def _():
        u_ref[...] = jnp.zeros_like(u_ref)
        zt_ref[...] = lax.dot_general(
            perm_ref[...], z_ref[0].astype(BF16), (((1,), (1,)), ((), ())), preferred_element_type=F32
        ).astype(BF16)

    w = ws_ref[...]
    for i, ref in enumerate((es_ref, et_ref)):
        u_ref[i] += lax.dot_general(
            ref[...], w, (((1,), (1,)), ((), ())), preferred_element_type=F32
        )


def combine_kernel(f_ref, u_ref, v_ref, own_ref, other_ref):
    for k in range(2):
        lanes = slice(k * 128, (k + 1) * 128)
        own_ref[:, lanes] = f_ref[0] * u_ref[0, :, lanes] - f_ref[1] * u_ref[1, :, lanes]
        other_ref[:, lanes] = f_ref[2] * v_ref[0, :, lanes] - f_ref[3] * v_ref[1, :, lanes]


def grad_kernel(blocks_ref, f_ref, eso_ref, eto_ref, esx_ref, etx_ref, zo_ref, zx_ref, ws_ref, inv_ref,
                own_ref, bp_ref, bm_ref, ap_ref, am_ref, g):
    for j, (s_ref, t_ref) in enumerate(((eso_ref, eto_ref), (esx_ref, etx_ref))):
        for k in range(TILE // 128):
            lanes = slice(k * 128, (k + 1) * 128)
            g[j, :, lanes] = (
                f_ref[2 * j] * s_ref[:, lanes].astype(F32)
                - f_ref[2 * j + 1] * t_ref[:, lanes].astype(F32)
            ).astype(BF16)
    grad = jnp.dot(zo_ref[...], g[0], preferred_element_type=F32)
    grad = grad + jnp.dot(zx_ref[...], g[1], preferred_element_type=F32)
    w = [ws_ref[pl.ds(pl.multiple_of(blocks_ref[i] * 16, 16), 16), :].astype(F32) for i in range(16)]
    dot = jnp.zeros((16, TILE), F32)
    for i in range(16):
        dot = dot + w[i] * grad[i * 16 : (i + 1) * 16]
    dot = jnp.sum(dot, axis=0, keepdims=True)
    inv = inv_ref[...]
    homes = (
        [(own_ref, i * 16) for i in range(4)]
        + [(bp_ref, i * 16) for i in range(4)]
        + [(bm_ref, i * 16) for i in range(4)]
        + [(ap_ref, 0), (ap_ref, 16), (am_ref, 0), (am_ref, 16)]
    )
    for i, (ref, at) in enumerate(homes):
        ref[at : at + 16, :] = (grad[i * 16 : (i + 1) * 16] - w[i] * dot) * inv


def ring_kernel(bp_ref, bm_ref, rp_ref, rm_ref, op_ref, om_ref):
    op_ref[0:32, :] = bp_ref[0:32, :] + rp_ref[...]
    op_ref[32:64, :] = bp_ref[32:64, :]
    om_ref[0:32, :] = bm_ref[0:32, :]
    om_ref[32:64, :] = bm_ref[32:64, :] + rm_ref[...]


def ring_end_kernel(own_ref, rp_ref, rm_ref, k_ref, c_ref, z_ref, zc_ref):
    for i, ref in enumerate((k_ref, c_ref, z_ref, zc_ref)):
        rows = slice(i * 16, (i + 1) * 16)
        ref[...] = own_ref[rows, :] + rp_ref[rows, :] + rm_ref[rows, :]


def protos_kernel(core_ref, *refs):
    out_ref = refs[-1]
    half = out_ref.shape[1] // 2
    mine = core_ref[0] * half
    theirs = (1 - core_ref[0]) * half
    at = 0
    for i, width in enumerate(CHUNKS):
        k_ref, c_ref, z_ref, zc_ref = refs[4 * i : 4 * i + 4]
        out_ref[:, pl.ds(pl.multiple_of(mine + at, 128), width)] = k_ref[...] + z_ref[...]
        out_ref[:, pl.ds(pl.multiple_of(theirs + at, 128), width)] = c_ref[...] + zc_ref[...]
        at += width


def split_kernel(x_ref, own_ref, got_ref, o0_ref, op_ref, om_ref, o2_ref):
    size = o0_ref.shape[0]
    for step, ref in ((0, o0_ref), (1, op_ref), (3, om_ref), (2, o2_ref)):
        rows = pl.ds(pl.multiple_of(lax.rem(x_ref[0] + step, 4) * size, 16), size)
        ref[...] = own_ref[rows, :] + got_ref[rows, :]


def sum4_kernel(a_ref, b_ref, c_ref, d_ref, out_ref):
    out_ref[...] = a_ref[...] + b_ref[...] + c_ref[...] + d_ref[...]


def rows_kernel(x_ref, a_ref, b_ref, c_ref, d_ref, rows_ref, out_ref):
    total = a_ref[...] + b_ref[...] + c_ref[...] + d_ref[...]
    size = out_ref.shape[0]
    v = rows_ref[pl.ds(pl.multiple_of(x_ref[0] * size, 16), size), :].astype(F32)
    norm = jnp.sqrt(jnp.sum(v * v, axis=1, keepdims=True) + norm_eps)
    z = v / norm
    out_ref[...] = (total - z * jnp.sum(z * total, axis=1, keepdims=True)) / norm


def place_kernel(x_ref, a_ref, p_ref, m_ref, t_ref, out_ref):
    size = a_ref.shape[0]
    for step, ref in ((0, a_ref), (3, p_ref), (1, m_ref), (2, t_ref)):
        rows = pl.ds(pl.multiple_of(lax.rem(x_ref[0] + step, 4) * size, 16), size)
        out_ref[rows, :] = ref[...]


def dp_pairs(move):
    def at(z, y, c):
        return (z * 4 + y) * 2 + c
    return [(at(z, y, c), at(*move(z, y, c))) for z in range(2) for y in range(4) for c in range(2)]


def mp_pairs(dx, dz):
    return [(x * 4 + z, (x + dx) % 4 * 4 + (z + dz) % 4) for x in range(4) for z in range(4)]


CORE = dp_pairs(lambda z, y, c: (z, y, 1 - c))
YP = dp_pairs(lambda z, y, c: (z, (y + 1) % 4, c))
YM = dp_pairs(lambda z, y, c: (z, (y - 1) % 4, c))
ZZ = dp_pairs(lambda z, y, c: (1 - z, y, c))
ZZC = dp_pairs(lambda z, y, c: (1 - z, y, 1 - c))


def to_dp(v, pairs):
    return lax.ppermute(v, "dp", pairs)


def to_mp(v, dx, dz):
    return lax.ppermute(v, "mp", mp_pairs(dx, dz))


def prefetch(grid, in_specs, out_specs, scratch=()):
    return pltpu.PrefetchScalarGridSpec(
        num_scalar_prefetch=1, grid=grid, in_specs=in_specs, out_specs=out_specs, scratch_shapes=scratch
    )


VM = pl.BlockSpec(memory_space=pltpu.VMEM)
SM = pl.BlockSpec(memory_space=pltpu.SMEM)


def local(student_rows, teacher_rows, student_protos, teacher_protos, center, row_weight):
    rows, feats = student_rows.shape
    protos = student_protos.shape[1]
    half = protos // 2
    dp = lax.axis_index("dp")
    core, y, z_hi = dp % 2, dp // 2 % 4, dp // 8
    x = lax.axis_index("mp") // 4
    core_s = core.astype(jnp.int32)[None]
    x_s = x.astype(jnp.int32)[None]
    blocks = jnp.stack([
        ((z_hi ^ zr) * 4 + (y + yr) % 4) * 2 + (core ^ cr)
        for yr in (0, 1, 3, 2) for zr in (0, 1) for cr in (0, 1)
    ]).astype(jnp.int32)
    source = jnp.repeat(blocks, 16) * 16 + jnp.arange(feats, dtype=jnp.int32) % 16
    perm = (source[:, None] == jnp.arange(feats, dtype=jnp.int32)[None, :]).astype(BF16)

    z = call(prep_kernel, shape((2, rows, feats)), student_rows, teacher_rows,
             in_specs=[VM, VM], out_specs=VM, nbytes=3 * MIB)
    z_other = to_dp(z, CORE)

    tiles = half // TILE
    center2 = center[None, :]
    weight2 = row_weight[None, :]
    z_spec = pl.BlockSpec((2, rows, feats), lambda i, c: (0, 0, 0))
    wide = lambda i, c: (0, c[0] * tiles + i)
    tile = lambda i, c: (0, i)
    fixed = lambda i, c: (0, 0)
    e_shape = shape((rows, half), BF16)
    e_spec = pl.BlockSpec((rows, TILE), tile)
    w_spec = pl.BlockSpec((feats, TILE), tile)
    pass_scratch = (pltpu.VMEM((2, rows, feats), BF16), pltpu.VMEM((2, rows, 128), F32))
    flops = 4 * rows * feats * half
    es_o, et_o, ws, wt, inv, sums = call(
        functools.partial(own_kernel, tiles - 1),
        (e_shape, e_shape, shape((feats, half), BF16), shape((feats, half), BF16), shape((1, half)), shape((2, rows))),
        core_s, z, student_protos, teacher_protos, center2,
        grid_spec=prefetch(
            (tiles,),
            [z_spec, pl.BlockSpec((feats, TILE), wide), pl.BlockSpec((feats, TILE), wide), pl.BlockSpec((1, TILE), wide)],
            [e_spec, e_spec, w_spec, w_spec, pl.BlockSpec((1, TILE), tile), pl.BlockSpec((2, rows), fixed)],
            pass_scratch,
        ),
        flops=flops, nbytes=20 * MIB,
    )
    es_x, et_x, pay = call(
        functools.partial(other_kernel, tiles - 1),
        (e_shape, e_shape, shape((8, rows))),
        core_s, z_other, ws, wt, center2, sums, weight2,
        grid_spec=prefetch(
            (tiles,),
            [z_spec, w_spec, w_spec, pl.BlockSpec((1, TILE), wide), pl.BlockSpec((2, rows), fixed), pl.BlockSpec((1, rows), fixed)],
            [e_spec, e_spec, pl.BlockSpec((8, rows), fixed)],
            pass_scratch,
        ),
        flops=flops, nbytes=20 * MIB,
    )
    small = dict(in_specs=[VM] * 2, out_specs=VM)
    small4 = dict(in_specs=[VM] * 4, out_specs=VM)
    tot = call(chip_kernel, shape((8, rows)), pay, to_dp(pay, CORE), **small)
    tot = call(add4_kernel, shape((8, rows)), tot, *[to_mp(tot, k, 0) for k in (1, 2, 3)], **small4)
    tot = [tot] + [to_mp(tot, 0, k) for k in (1, 2, 3)]

    def unit(es, et, zz):
        ut = 2 * TILE
        return call(
            unit_kernel, (shape((2, rows, feats)), shape((feats, rows), BF16)), es, et, ws, zz, perm,
            grid=(half // ut,),
            in_specs=[
                pl.BlockSpec((rows, ut), lambda i: (0, i)), pl.BlockSpec((rows, ut), lambda i: (0, i)),
                pl.BlockSpec((feats, ut), lambda i: (0, i)), pl.BlockSpec((1, rows, feats), lambda i: (0, 0, 0)),
                pl.BlockSpec((feats, feats), lambda i: (0, 0)),
            ],
            out_specs=[pl.BlockSpec((2, rows, feats), lambda i: (0, 0, 0)), pl.BlockSpec((feats, rows), lambda i: (0, 0))],
            flops=flops, nbytes=18 * MIB,
        )

    u_o, zt_o = unit(es_o, et_o, z)
    u_x, zt_x = unit(es_x, et_x, z_other)
    f = call(factors_kernel, shape((4, rows, 128)), *tot, **small4)

    def chunk(at, width):
        first = at // TILE
        t = lambda i, b: (0, first + i)
        o = lambda i, b: (0, i)
        e = pl.BlockSpec((rows, TILE), t)
        zt = pl.BlockSpec((feats, rows), lambda i, b: (0, 0))
        return call(
            grad_kernel, (*[shape((64, width))] * 3, *[shape((32, width))] * 2),
            blocks, f, es_o, et_o, es_x, et_x, zt_o, zt_x, ws, inv,
            grid_spec=prefetch(
                (width // TILE,),
                [pl.BlockSpec((4, rows, 128), lambda i, b: (0, 0, 0)), e, e, e, e, zt, zt,
                 pl.BlockSpec((feats, TILE), t), pl.BlockSpec((1, TILE), t)],
                [pl.BlockSpec((64, TILE), o)] * 3 + [pl.BlockSpec((32, TILE), o)] * 2,
                (pltpu.VMEM((2, rows, TILE), BF16),),
            ),
            flops=flops * width // half, nbytes=26 * MIB * width // half,
        )

    parts = []
    at = 0
    for width in CHUNKS:
        own, bp, bm, ap, am = chunk(at, width)
        bp, bm = call(ring_kernel, (shape((64, width)),) * 2, bp, bm, to_dp(ap, YP), to_dp(am, YM),
                      in_specs=[VM] * 4, out_specs=[VM] * 2, input_output_aliases={0: 0, 1: 1})
        keep, c, zz, zc = call(ring_end_kernel, (shape((16, width)),) * 4, own, to_dp(bp, YP), to_dp(bm, YM),
                               in_specs=[VM] * 3, out_specs=[VM] * 4)
        parts += [keep, to_dp(c, CORE), to_dp(zz, ZZ), to_dp(zc, ZZC)]
        at += width

    g_own, g_other = call(combine_kernel, (shape((rows, feats)),) * 2, f, u_o, u_x,
                          in_specs=[VM] * 3, out_specs=[VM] * 2)
    quarter = shape((rows // 4, feats))
    o0, op, om, o2 = call(split_kernel, (quarter,) * 4, x_s, g_own, to_dp(g_other, CORE),
                          in_specs=[SM, VM, VM], out_specs=[VM] * 4)
    part = call(sum4_kernel, quarter, o0, to_mp(op, 1, 0), to_mp(om, 3, 0), to_mp(o2, 2, 0), **small4)
    mine = call(rows_kernel, quarter, x_s, part, *[to_mp(part, 0, k) for k in (1, 2, 3)], student_rows,
                in_specs=[SM] + [VM] * 5, out_specs=VM)
    grad_rows = call(place_kernel, shape((rows, feats)), x_s, mine, to_mp(mine, 1, 0), to_mp(mine, 3, 0), to_mp(mine, 2, 0),
                     in_specs=[SM] + [VM] * 4, out_specs=VM)
    proto_grad = call(protos_kernel, shape((16, protos)), core_s, *parts,
                      in_specs=[SM] + [VM] * len(parts), out_specs=VM)
    return grad_rows, proto_grad


def solution(mesh):
    placed = (P("dp", None), P("dp", None), P(None, "mp"), P(None, "mp"), P("mp"), P("dp"))
    return jax.shard_map(
        local, mesh=mesh, in_specs=placed, out_specs=(P("dp", None), P("dp", "mp")), check_vma=False
    )
```

```python
import functools
import jax
import jax.numpy as jnp
import numpy as np
from jax import lax
from jax.experimental import pallas as pl
from jax.experimental.pallas import tpu as pltpu
from jax.sharding import PartitionSpec as P

student_temp = 0.1
teacher_temp = 0.04
norm_eps = 1e-06
LOG2E = 1.4426950408889634
F32 = jnp.float32
BF16 = jnp.bfloat16
TILE = 1024
ROWBLK = 768
PART = 512
CHUNKS = (2048, 2048)
MIB = 1 << 20


def call(kernel, out, *args, in_specs, out_specs, after=(), scalars=0, grid=(), scratch_shapes=(), aliases=None,
         vmem=8, flops=0, nbytes=0):
    count, extra = len(args), len(after)

    def body(*refs):
        kernel(*refs[:count], *refs[count + extra :])

    return pl.pallas_call(
        body,
        out_shape=out,
        grid_spec=pltpu.PrefetchScalarGridSpec(
            num_scalar_prefetch=scalars,
            grid=grid,
            in_specs=list(in_specs) + [pl.BlockSpec(memory_space=pl.ANY)] * extra,
            out_specs=out_specs,
            scratch_shapes=scratch_shapes,
        ),
        input_output_aliases=aliases or {},
        compiler_params=pltpu.CompilerParams(vmem_limit_bytes=vmem * MIB),
        cost_estimate=pl.CostEstimate(flops=flops, bytes_accessed=nbytes, transcendentals=0),
    )(*args, *after)


def shape(dims, dtype=F32):
    return jax.ShapeDtypeStruct(dims, dtype)


def prep_kernel(s_ref, t_ref, z_ref):
    size = s_ref.shape[0]
    rows = pl.ds(pl.multiple_of(pl.program_id(0) * size, size), size)
    for i, ref in enumerate((s_ref, t_ref)):
        v = ref[...].astype(F32)
        z_ref[i, rows, :] = v / jnp.sqrt(jnp.sum(v * v, axis=1, keepdims=True) + norm_eps)


def unit_columns(ref):
    v = ref[...].astype(F32)
    inv = 1.0 / jnp.sqrt(jnp.sum(v * v, axis=0, keepdims=True) + norm_eps)
    return (v * inv).astype(BF16), inv


def tile_at(i):
    return pl.ds(pl.multiple_of(i * TILE, TILE), TILE)


def logits_pass(z_ref, ws_ref, wt_ref, center_ref, es_ref, et_ref, sums_ref, zb, acc, last):
    @pl.when(pl.program_id(0) == 0)
    def _():
        zb[...] = z_ref[...].astype(BF16)
        acc[...] = jnp.zeros_like(acc)

    cols = tile_at(pl.program_id(0))
    shift = center_ref[...] * (LOG2E / teacher_temp)
    rows = zb.shape[1]
    for r in range(rows // ROWBLK):
        part = pl.ds(r * ROWBLK, ROWBLK)
        for i, (w_ref, e_ref) in enumerate(((ws_ref, es_ref), (wt_ref, et_ref))):
            logit = jnp.dot(zb[i, part, :], w_ref[:, cols], preferred_element_type=F32)
            if i == 0:
                e = jnp.exp2(logit * (LOG2E / student_temp))
            else:
                e = jnp.exp2(logit * (LOG2E / teacher_temp) - shift)
            total = e[:, :128]
            for k in range(1, TILE // 128):
                total = total + e[:, k * 128 : (k + 1) * 128]
            acc[i, part, :] += total
            e_ref[part, cols] = e.astype(BF16)

    @pl.when(pl.program_id(0) == last)
    def _():
        for i in range(2):
            sums_ref[i : i + 1, :] = jnp.sum(acc[i].T, axis=0, keepdims=True)


def own_kernel(last, core_ref, z_ref, sp_ref, tp_ref, center_ref,
               es_ref, et_ref, ws_ref, wt_ref, inv_ref, sums_ref, zb, acc):
    cols = tile_at(pl.program_id(0))
    w_s, inv = unit_columns(sp_ref)
    w_t, _ = unit_columns(tp_ref)
    ws_ref[:, cols] = w_s
    wt_ref[:, cols] = w_t
    inv_ref[:, cols] = inv
    logits_pass(z_ref, ws_ref, wt_ref, center_ref, es_ref, et_ref, sums_ref, zb, acc, last)


def other_kernel(last, core_ref, z_ref, ws_ref, wt_ref, center_ref, mine_ref, weight_ref,
                 es_ref, et_ref, pay_ref, zb, acc):
    logits_pass(z_ref, ws_ref, wt_ref, center_ref, es_ref, et_ref, pay_ref.at[2:4], zb, acc, last)

    @pl.when(pl.program_id(0) == 0)
    def _():
        pay_ref[0:2, :] = mine_ref[...]
        pay_ref[4:5, :] = weight_ref[...]
        pay_ref[5:8, :] = jnp.zeros_like(pay_ref[5:8, :])


def chip_kernel(mine_ref, theirs_ref, out_ref):
    out_ref[0:2, :] = mine_ref[0:2, :] + theirs_ref[2:4, :]
    out_ref[2:4, :] = mine_ref[2:4, :] + theirs_ref[0:2, :]
    out_ref[4:5, :] = mine_ref[4:5, :]
    out_ref[5:6, :] = theirs_ref[4:5, :]
    out_ref[6:8, :] = jnp.zeros_like(out_ref[6:8, :])


def add4_kernel(a_ref, b_ref, c_ref, d_ref, out_ref):
    out_ref[0:4, :] = a_ref[0:4, :] + b_ref[0:4, :] + c_ref[0:4, :] + d_ref[0:4, :]
    out_ref[4:8, :] = a_ref[4:8, :]


def scale_kernel(a_ref, b_ref, c_ref, d_ref, zo_ref, zx_ref, u_ref, out_ref, f_ref, mix_ref, fac):
    total = a_ref[0:4, :] + b_ref[0:4, :] + c_ref[0:4, :] + d_ref[0:4, :]
    rows = total.shape[1]
    for i in range(4):
        weight = a_ref[4 + i // 2 : 5 + i // 2, :]
        f = weight / (total[i : i + 1, :] * student_temp)
        if i % 2:
            f = -f
        f_ref[i : i + 1, :] = f
        z_ref = zo_ref if i < 2 else zx_ref
        out_ref[:, i * rows : (i + 1) * rows] = (z_ref[...].astype(F32) * f).astype(BF16)
    mix_kernel(f_ref, u_ref, mix_ref, fac)


def unit_kernel(es_ref, et_ref, ws_ref, z_ref, perm_ref, u_ref, zt_ref):
    zt_ref[...] = lax.dot_general(
        perm_ref[...], z_ref[0].astype(BF16), (((1,), (1,)), ((), ())), preferred_element_type=F32
    ).astype(BF16)
    for i, ref in enumerate((es_ref, et_ref)):
        u_ref[i] = lax.dot_general(
            ref[...], ws_ref[...], (((1,), (1,)), ((), ())), preferred_element_type=F32
        )


def fill_columns(f_ref, first, fac):
    for i in range(2):
        fac[i] = jnp.broadcast_to(f_ref[first + i : first + i + 1, :], (128, fac.shape[1])).T


def mix_kernel(f_ref, u_ref, out_ref, fac):
    fill_columns(f_ref, 2, fac)
    for k in range(2):
        lanes = slice(k * 128, (k + 1) * 128)
        out_ref[:, lanes] = fac[0] * u_ref[0, :, lanes] + fac[1] * u_ref[1, :, lanes]


def combine_kernel(x_ref, f_ref, u_ref, got_ref, o0_ref, op_ref, om_ref, o2_ref, fac):
    fill_columns(f_ref, 0, fac)
    size = o0_ref.shape[0]
    for step, ref in ((0, o0_ref), (1, op_ref), (3, om_ref), (2, o2_ref)):
        rows = pl.ds(pl.multiple_of(lax.rem(x_ref[0] + step, 4) * size, 16), size)
        for k in range(2):
            lanes = slice(k * 128, (k + 1) * 128)
            ref[:, lanes] = (
                fac[0, rows, :] * u_ref[0, rows, lanes] + fac[1, rows, :] * u_ref[1, rows, lanes]
            ) + got_ref[rows, lanes]


def grad_kernel(blocks_ref, z_ref, eso_ref, eto_ref, esx_ref, etx_ref, ws_ref, inv_ref,
                own_ref, bp_ref, bm_ref, ap_ref, am_ref):
    rows = eso_ref.shape[0]
    grad = None
    for i, ref in enumerate((eso_ref, eto_ref, esx_ref, etx_ref)):
        term = jnp.dot(z_ref[:, i * rows : (i + 1) * rows], ref[...], preferred_element_type=F32)
        grad = term if grad is None else grad + term
    w = [ws_ref[pl.ds(pl.multiple_of(blocks_ref[i] * 16, 16), 16), :].astype(F32) for i in range(16)]
    dot = w[0] * grad[0:16]
    for i in range(1, 16):
        dot = dot + w[i] * grad[i * 16 : (i + 1) * 16]
    dot = jnp.sum(dot, axis=0, keepdims=True)
    inv = inv_ref[...]
    homes = (
        [(own_ref, i * 16) for i in range(4)]
        + [(bp_ref, i * 16) for i in range(4)]
        + [(bm_ref, i * 16) for i in range(4)]
        + [(ap_ref, 0), (ap_ref, 16), (am_ref, 0), (am_ref, 16)]
    )
    for i, (ref, at) in enumerate(homes):
        ref[at : at + 16, :] = (grad[i * 16 : (i + 1) * 16] - w[i] * dot) * inv


def ring_kernel(bp_ref, bm_ref, ap_ref, am_ref, rp_ref, rm_ref, op_ref, om_ref):
    op_ref[0:32, :] = bp_ref[0:32, :] + rp_ref[...]
    op_ref[32:64, :] = bp_ref[32:64, :]
    op_ref[64:96, :] = ap_ref[...]
    om_ref[0:32, :] = bm_ref[0:32, :]
    om_ref[32:64, :] = bm_ref[32:64, :] + rm_ref[...]
    om_ref[64:96, :] = am_ref[...]


def ring_last_kernel(bp_ref, bm_ref, rp_ref, rm_ref, op_ref, om_ref):
    op_ref[0:32, :] = bp_ref[0:32, :] + rp_ref[64:96, :]
    op_ref[32:64, :] = bp_ref[32:64, :]
    om_ref[0:32, :] = bm_ref[0:32, :]
    om_ref[32:64, :] = bm_ref[32:64, :] + rm_ref[64:96, :]


def ring_end_kernel(own_ref, rp_ref, rm_ref, k_ref, c_ref, z_ref):
    for at, ref in ((0, k_ref), (16, c_ref), (32, z_ref)):
        rows = slice(at, at + ref.shape[0])
        ref[...] = own_ref[rows, :] + rp_ref[rows, :] + rm_ref[rows, :]


def ring_end_last_kernel(own_ref, rp_ref, rm_ref, before_ref, got_ref, k_ref, c_ref, z_ref, zc_ref):
    width = k_ref.shape[1]
    c_ref[:, 0 : before_ref.shape[1]] = before_ref[...] + got_ref[16:32, :]
    for i, ref in enumerate((k_ref, c_ref.at[:, c_ref.shape[1] - width :], z_ref, zc_ref)):
        rows = slice(i * 16, (i + 1) * 16)
        ref[...] = own_ref[rows, :] + rp_ref[rows, :] + rm_ref[rows, :]


def protos_kernel(core_ref, k0_ref, z0_ref, k1_ref, z1_ref, x1_ref, c_ref, out_ref):
    half = out_ref.shape[1] // 2
    at = k0_ref.shape[1]
    mine = core_ref[0] * half
    theirs = (1 - core_ref[0]) * half
    columns = lambda start, width: pl.ds(pl.multiple_of(start, 128), width)
    out_ref[:, columns(mine, at)] = k0_ref[...] + z0_ref[0:16, :]
    out_ref[:, columns(theirs, at)] = c_ref[:, 0:at]
    out_ref[:, columns(mine + at, half - at)] = k1_ref[...] + z1_ref[...]
    out_ref[:, columns(theirs + at, half - at)] = c_ref[:, at:half] + x1_ref[...]


def sum4_kernel(a_ref, b_ref, c_ref, d_ref, out_ref):
    out_ref[...] = a_ref[...] + b_ref[...] + c_ref[...] + d_ref[...]


def rows_kernel(x_ref, a_ref, b_ref, c_ref, d_ref, rows_ref, out_ref):
    total = a_ref[...] + b_ref[...] + c_ref[...] + d_ref[...]
    v = rows_ref[...].astype(F32)
    norm = jnp.sqrt(jnp.sum(v * v, axis=1, keepdims=True) + norm_eps)
    z = v / norm
    out_ref[...] = (total - z * jnp.sum(z * total, axis=1, keepdims=True)) / norm


def place_kernel(x_ref, a_ref, p_ref, m_ref, t_ref, out_ref):
    size = a_ref.shape[0]
    for step, ref in ((0, a_ref), (3, p_ref), (1, m_ref), (2, t_ref)):
        rows = pl.ds(pl.multiple_of(lax.rem(x_ref[0] + step, 4) * size, 16), size)
        out_ref[rows, :] = ref[...]


def dp_pairs(move):
    def at(z, y, c):
        return (z * 4 + y) * 2 + c
    return [(at(z, y, c), at(*move(z, y, c))) for z in range(2) for y in range(4) for c in range(2)]


def mp_pairs(dx, dz):
    return [(x * 4 + z, (x + dx) % 4 * 4 + (z + dz) % 4) for x in range(4) for z in range(4)]


CORE = dp_pairs(lambda z, y, c: (z, y, 1 - c))
YP = dp_pairs(lambda z, y, c: (z, (y + 1) % 4, c))
YM = dp_pairs(lambda z, y, c: (z, (y - 1) % 4, c))
ZZ = dp_pairs(lambda z, y, c: (1 - z, y, c))
ZZC = dp_pairs(lambda z, y, c: (1 - z, y, 1 - c))


def to_dp(v, pairs):
    return lax.ppermute(v, "dp", pairs)


def to_mp(v, dx, dz):
    return lax.ppermute(v, "mp", mp_pairs(dx, dz))


VM = pl.BlockSpec(memory_space=pltpu.VMEM)
SM = pl.BlockSpec(memory_space=pltpu.SMEM)


def local(student_rows, teacher_rows, student_protos, teacher_protos, center, row_weight):
    rows, feats = student_rows.shape
    protos = student_protos.shape[1]
    half = protos // 2
    dp = lax.axis_index("dp")
    core, y, z_hi = dp % 2, dp // 2 % 4, dp // 8
    x = lax.axis_index("mp") // 4
    core_s = core.astype(jnp.int32)[None]
    x_s = x.astype(jnp.int32)[None]
    blocks = jnp.stack([
        ((z_hi ^ zr) * 4 + (y + yr) % 4) * 2 + (core ^ cr)
        for yr in (0, 1, 3, 2) for zr in (0, 1) for cr in (0, 1)
    ]).astype(jnp.int32)
    source = jnp.repeat(blocks, 16) * 16 + jnp.arange(feats, dtype=jnp.int32) % 16
    perm = (source[:, None] == jnp.arange(feats, dtype=jnp.int32)[None, :]).astype(BF16)
    hbm = lambda v: pltpu.with_memory_space_constraint(v, pltpu.HBM)

    row_tile = pl.BlockSpec((rows // 2, feats), lambda i: (i, 0))
    z = call(prep_kernel, shape((2, rows, feats)), hbm(student_rows), hbm(teacher_rows), grid=(2,),
             in_specs=[row_tile, row_tile], out_specs=VM, nbytes=3 * MIB)
    z_other = to_dp(z, CORE)

    tiles = half // TILE
    center2 = center[None, :]
    weight2 = row_weight[None, :]
    wide = lambda i, c: (0, c[0] * tiles + i)
    w_wide = pl.BlockSpec((feats, TILE), wide)
    e_shape = pltpu.VMEM((rows, half), BF16)
    w_shape = shape((feats, half), BF16)
    pass_scratch = (pltpu.VMEM((2, rows, feats), BF16), pltpu.VMEM((2, rows, 128), F32))
    flops = 4 * rows * feats * half
    es_o, et_o, ws, wt, inv, sums = call(
        functools.partial(own_kernel, tiles - 1),
        (e_shape, e_shape, w_shape, w_shape, shape((1, half)), shape((2, rows))),
        core_s, z, hbm(student_protos), hbm(teacher_protos), center2,
        scalars=1, grid=(tiles,), in_specs=[VM, w_wide, w_wide, pl.BlockSpec((1, TILE), wide)],
        out_specs=[VM] * 6, scratch_shapes=pass_scratch,
        vmem=14, flops=flops, nbytes=8 * MIB,
    )
    es_x, et_x, pay = call(
        functools.partial(other_kernel, tiles - 1),
        (e_shape, e_shape, shape((8, rows))),
        core_s, z_other, ws, wt, center2, sums, weight2,
        scalars=1, grid=(tiles,), in_specs=[VM, VM, VM, pl.BlockSpec((1, TILE), wide), VM, VM],
        out_specs=[VM] * 3, scratch_shapes=pass_scratch,
        vmem=14, flops=flops, nbytes=8 * MIB,
    )
    small = dict(in_specs=[VM] * 2, out_specs=VM)
    small4 = dict(in_specs=[VM] * 4, out_specs=VM)

    tot1 = call(chip_kernel, shape((8, rows)), pay, to_dp(pay, CORE), **small)
    tot2 = call(add4_kernel, shape((8, rows)), tot1, *[to_mp(tot1, k, 0) for k in (1, 2, 3)], **small4)
    tot = [tot2] + [to_mp(tot2, 0, k) for k in (1, 2, 3)]

    def unit(es, et, zz, after):
        return call(
            unit_kernel, (shape((2, rows, feats)), shape((feats, rows), BF16)), es, et, ws, zz, perm,
            in_specs=[VM] * 5, out_specs=[VM] * 2, after=after, vmem=16, flops=flops, nbytes=8 * MIB,
        )

    u_x, zt_x = unit(es_x, et_x, z_other, (tot1,))
    u_o, zt_o = unit(es_o, et_o, z, (tot2,))
    fac = [pltpu.VMEM((2, rows, 128), F32)]
    zs, f, mixed = call(scale_kernel, (shape((feats, 4 * rows), BF16), shape((4, rows)), shape((rows, feats))), *tot, zt_o, zt_x, u_x,
                        in_specs=[VM] * 7, out_specs=[VM] * 3, scratch_shapes=fac)
    got = to_dp(mixed, CORE)

    def chunk(at, width, after):
        first = at // PART
        own = lambda i, b: (0, i)
        col = lambda i, b: (0, first + i)
        e_tile = pl.BlockSpec((rows, PART), col)
        return call(
            grad_kernel, (*[shape((64, width))] * 3, *[shape((32, width))] * 2),
            blocks, zs, hbm(es_o), hbm(et_o), hbm(es_x), hbm(et_x), ws, inv,
            scalars=1, grid=(width // PART,),
            in_specs=[VM] + [e_tile] * 4 + [pl.BlockSpec((feats, PART), col), pl.BlockSpec((1, PART), col)],
            out_specs=[pl.BlockSpec((64, PART), own)] * 3 + [pl.BlockSpec((32, PART), own)] * 2,
            after=after, vmem=24, flops=2 * flops * width // half, nbytes=26 * MIB * width // half,
        )

    quarter = shape((rows // 4, feats))
    w0, w1 = CHUNKS
    own0, bp0, bm0, ap0, am0 = chunk(0, w0, ())
    o0, op, om, o2 = call(combine_kernel, (quarter,) * 4, x_s, f, u_o, got, after=(ap0,),
                          in_specs=[SM, VM, VM, VM], out_specs=[VM] * 4, scratch_shapes=fac)
    own1, bp1, bm1, ap1, am1 = chunk(w0, w1, (o0,))
    part = call(sum4_kernel, quarter, o0, to_mp(op, 1, 0), to_mp(om, 3, 0), to_mp(o2, 2, 0), **small4)
    mp, mm = call(ring_kernel, (shape((96, w0)),) * 2, bp0, bm0, ap1, am1, to_dp(ap0, YP), to_dp(am0, YM),
                  after=(part,), in_specs=[VM] * 6, out_specs=[VM] * 2)
    gp, gm = to_dp(mp, YP), to_dp(mm, YM)
    fixed = pl.BlockSpec((rows // 4, feats), lambda i, c: (0, 0))
    mine = call(rows_kernel, quarter, x_s, part, *[to_mp(part, 0, k) for k in (1, 2, 3)], hbm(student_rows),
                scalars=1, grid=(1,), in_specs=[fixed] * 4 + [pl.BlockSpec((rows // 4, feats), lambda i, c: (c[0], 0))],
                out_specs=fixed)
    bp1, bm1 = call(ring_last_kernel, (shape((64, w1)),) * 2, bp1, bm1, gp, gm, after=(mine,),
                    in_specs=[VM] * 4, out_specs=[VM] * 2)
    keep0, c0, zz0 = call(ring_end_kernel, (shape((16, w0)), shape((16, w0)), shape((32, w0))), own0, gp, gm,
                          after=(bp1,), in_specs=[VM] * 3, out_specs=[VM] * 3)
    got0 = to_dp(zz0, ZZ)
    keep1, c1, zz1, zc1 = call(
        ring_end_last_kernel, (shape((16, w1)), shape((16, half)), shape((16, w1)), shape((16, w1))),
        own1, to_dp(bp1, YP), to_dp(bm1, YM), c0, got0, in_specs=[VM] * 5, out_specs=[VM] * 4)
    parts = [keep0, got0, keep1, to_dp(zz1, ZZ), to_dp(zc1, ZZC), to_dp(c1, CORE)]
    grad_rows = call(place_kernel, shape((rows, feats)), x_s, mine, to_mp(mine, 1, 0), to_mp(mine, 3, 0), to_mp(mine, 2, 0),
                     in_specs=[SM] + [VM] * 4, out_specs=VM)
    proto_grad = call(protos_kernel, shape((16, protos)), core_s, *parts,
                      in_specs=[SM] + [VM] * len(parts), out_specs=VM)
    return grad_rows, proto_grad


def solution(mesh):
    placed = (P("dp", None), P("dp", None), P(None, "mp"), P(None, "mp"), P("mp"), P("dp"))
    return jax.shard_map(
        local, mesh=mesh, in_specs=placed, out_specs=(P("dp", None), P("dp", "mp")), check_vma=False
    )
```

```python
import functools
import jax
import jax.numpy as jnp
import numpy as np
from jax import lax
from jax.experimental import pallas as pl
from jax.experimental.pallas import tpu as pltpu
from jax.sharding import PartitionSpec as P

student_temp = 0.1
teacher_temp = 0.04
norm_eps = 1e-06
LOG2E = 1.4426950408889634
F32 = jnp.float32
BF16 = jnp.bfloat16
TILE = 1024
ROWBLK = 768
PART = 512
CHUNKS = (2048, 2048)
MIB = 1 << 20


def call(kernel, out, *args, in_specs, out_specs, after=(), scalars=0, grid=(), scratch_shapes=(), aliases=None,
         vmem=8, flops=0, nbytes=0):
    count, extra = len(args), len(after)

    def body(*refs):
        kernel(*refs[:count], *refs[count + extra :])

    return pl.pallas_call(
        body,
        out_shape=out,
        grid_spec=pltpu.PrefetchScalarGridSpec(
            num_scalar_prefetch=scalars,
            grid=grid,
            in_specs=list(in_specs) + [pl.BlockSpec(memory_space=pl.ANY)] * extra,
            out_specs=out_specs,
            scratch_shapes=scratch_shapes,
        ),
        input_output_aliases=aliases or {},
        compiler_params=pltpu.CompilerParams(vmem_limit_bytes=vmem * MIB),
        cost_estimate=pl.CostEstimate(flops=flops, bytes_accessed=nbytes, transcendentals=0),
    )(*args, *after)


def shape(dims, dtype=F32):
    return jax.ShapeDtypeStruct(dims, dtype)


def prep_kernel(s_ref, t_ref, z_ref):
    size = s_ref.shape[0]
    rows = pl.ds(pl.multiple_of(pl.program_id(0) * size, size), size)
    for i, ref in enumerate((s_ref, t_ref)):
        v = ref[...].astype(F32)
        z_ref[i, rows, :] = v / jnp.sqrt(jnp.sum(v * v, axis=1, keepdims=True) + norm_eps)


def unit_columns(ref):
    v = ref[...].astype(F32)
    inv = 1.0 / jnp.sqrt(jnp.sum(v * v, axis=0, keepdims=True) + norm_eps)
    return (v * inv).astype(BF16), inv


def tile_at(i):
    return pl.ds(pl.multiple_of(i * TILE, TILE), TILE)


def logits_pass(z_ref, ws_ref, wt_ref, center_ref, es_ref, et_ref, sums_ref, zb, acc, last):
    @pl.when(pl.program_id(0) == 0)
    def _():
        zb[...] = z_ref[...].astype(BF16)
        acc[...] = jnp.zeros_like(acc)

    cols = tile_at(pl.program_id(0))
    shift = center_ref[...] * (LOG2E / teacher_temp)
    rows = zb.shape[1]
    for r in range(rows // ROWBLK):
        part = pl.ds(r * ROWBLK, ROWBLK)
        for i, (w_ref, e_ref) in enumerate(((ws_ref, es_ref), (wt_ref, et_ref))):
            logit = jnp.dot(zb[i, part, :], w_ref[:, cols], preferred_element_type=F32)
            if i == 0:
                e = jnp.exp2(logit * (LOG2E / student_temp))
            else:
                e = jnp.exp2(logit * (LOG2E / teacher_temp) - shift)
            total = e[:, :128]
            for k in range(1, TILE // 128):
                total = total + e[:, k * 128 : (k + 1) * 128]
            acc[i, part, :] += total
            e_ref[part, cols] = e.astype(BF16)

    @pl.when(pl.program_id(0) == last)
    def _():
        for i in range(2):
            sums_ref[i : i + 1, :] = jnp.sum(acc[i].T, axis=0, keepdims=True)


def own_kernel(last, core_ref, z_ref, sp_ref, tp_ref, center_ref,
               es_ref, et_ref, ws_ref, wt_ref, inv_ref, sums_ref, zb, acc):
    cols = tile_at(pl.program_id(0))
    w_s, inv = unit_columns(sp_ref)
    w_t, _ = unit_columns(tp_ref)
    ws_ref[:, cols] = w_s
    wt_ref[:, cols] = w_t
    inv_ref[:, cols] = inv
    logits_pass(z_ref, ws_ref, wt_ref, center_ref, es_ref, et_ref, sums_ref, zb, acc, last)


def other_kernel(last, core_ref, z_ref, ws_ref, wt_ref, center_ref, mine_ref, weight_ref,
                 es_ref, et_ref, pay_ref, zb, acc):
    logits_pass(z_ref, ws_ref, wt_ref, center_ref, es_ref, et_ref, pay_ref.at[2:4], zb, acc, last)

    @pl.when(pl.program_id(0) == 0)
    def _():
        pay_ref[0:2, :] = mine_ref[...]
        pay_ref[4:5, :] = weight_ref[...]
        pay_ref[5:8, :] = jnp.zeros_like(pay_ref[5:8, :])


def chip_kernel(mine_ref, theirs_ref, out_ref):
    out_ref[0:2, :] = mine_ref[0:2, :] + theirs_ref[2:4, :]
    out_ref[2:4, :] = mine_ref[2:4, :] + theirs_ref[0:2, :]
    out_ref[4:5, :] = mine_ref[4:5, :]
    out_ref[5:6, :] = theirs_ref[4:5, :]
    out_ref[6:8, :] = jnp.zeros_like(out_ref[6:8, :])


def add4_kernel(a_ref, b_ref, c_ref, d_ref, out_ref):
    out_ref[0:4, :] = a_ref[0:4, :] + b_ref[0:4, :] + c_ref[0:4, :] + d_ref[0:4, :]
    out_ref[4:8, :] = a_ref[4:8, :]


def scale_kernel(a_ref, b_ref, c_ref, d_ref, zo_ref, zx_ref, u_ref, out_ref, f_ref, mix_ref, fac):
    total = a_ref[0:4, :] + b_ref[0:4, :] + c_ref[0:4, :] + d_ref[0:4, :]
    rows = total.shape[1]
    for i in range(4):
        weight = a_ref[4 + i // 2 : 5 + i // 2, :]
        f = weight / (total[i : i + 1, :] * student_temp)
        if i % 2:
            f = -f
        f_ref[i : i + 1, :] = f
        z_ref = zo_ref if i < 2 else zx_ref
        out_ref[:, i * rows : (i + 1) * rows] = (z_ref[...].astype(F32) * f).astype(BF16)
    mix_kernel(f_ref, u_ref, mix_ref, fac)


def unit_kernel(es_ref, et_ref, ws_ref, z_ref, perm_ref, u_ref, zt_ref):
    zt_ref[...] = lax.dot_general(
        perm_ref[...], z_ref[0].astype(BF16), (((1,), (1,)), ((), ())), preferred_element_type=F32
    ).astype(BF16)
    for i, ref in enumerate((es_ref, et_ref)):
        u_ref[i] = lax.dot_general(
            ref[...], ws_ref[...], (((1,), (1,)), ((), ())), preferred_element_type=F32
        )


def fill_columns(f_ref, first, fac):
    for i in range(2):
        fac[i] = jnp.broadcast_to(f_ref[first + i : first + i + 1, :], (128, fac.shape[1])).T


def mix_kernel(f_ref, u_ref, out_ref, fac):
    fill_columns(f_ref, 2, fac)
    for k in range(2):
        lanes = slice(k * 128, (k + 1) * 128)
        out_ref[:, lanes] = fac[0] * u_ref[0, :, lanes] + fac[1] * u_ref[1, :, lanes]


def combine_kernel(x_ref, f_ref, u_ref, got_ref, o0_ref, op_ref, om_ref, o2_ref, fac):
    fill_columns(f_ref, 0, fac)
    size = o0_ref.shape[0]
    for step, ref in ((0, o0_ref), (1, op_ref), (3, om_ref), (2, o2_ref)):
        rows = pl.ds(pl.multiple_of(lax.rem(x_ref[0] + step, 4) * size, 16), size)
        for k in range(2):
            lanes = slice(k * 128, (k + 1) * 128)
            ref[:, lanes] = (
                fac[0, rows, :] * u_ref[0, rows, lanes] + fac[1, rows, :] * u_ref[1, rows, lanes]
            ) + got_ref[rows, lanes]


def grad_kernel(blocks_ref, z_ref, eso_ref, eto_ref, esx_ref, etx_ref, ws_ref, inv_ref,
                own_ref, bp_ref, bm_ref, ap_ref, am_ref):
    rows = eso_ref.shape[0]
    grad = None
    for i, ref in enumerate((eso_ref, eto_ref, esx_ref, etx_ref)):
        term = jnp.dot(z_ref[:, i * rows : (i + 1) * rows], ref[...], preferred_element_type=F32)
        grad = term if grad is None else grad + term
    w = [ws_ref[pl.ds(pl.multiple_of(blocks_ref[i] * 16, 16), 16), :].astype(F32) for i in range(16)]
    dot = w[0] * grad[0:16]
    for i in range(1, 16):
        dot = dot + w[i] * grad[i * 16 : (i + 1) * 16]
    dot = jnp.sum(dot, axis=0, keepdims=True)
    inv = inv_ref[...]
    homes = (
        [(own_ref, i * 16) for i in range(4)]
        + [(bp_ref, i * 16) for i in range(4)]
        + [(bm_ref, i * 16) for i in range(4)]
        + [(ap_ref, 0), (ap_ref, 16), (am_ref, 0), (am_ref, 16)]
    )
    for i, (ref, at) in enumerate(homes):
        ref[at : at + 16, :] = (grad[i * 16 : (i + 1) * 16] - w[i] * dot) * inv


def ring_kernel(bp_ref, bm_ref, ap_ref, am_ref, rp_ref, rm_ref, op_ref, om_ref):
    op_ref[0:32, :] = bp_ref[0:32, :] + rp_ref[...]
    op_ref[32:64, :] = bp_ref[32:64, :]
    op_ref[64:96, :] = ap_ref[...]
    om_ref[0:32, :] = bm_ref[0:32, :]
    om_ref[32:64, :] = bm_ref[32:64, :] + rm_ref[...]
    om_ref[64:96, :] = am_ref[...]


def ring_last_kernel(bp_ref, bm_ref, rp_ref, rm_ref, op_ref, om_ref):
    op_ref[0:32, :] = bp_ref[0:32, :] + rp_ref[64:96, :]
    op_ref[32:64, :] = bp_ref[32:64, :]
    om_ref[0:32, :] = bm_ref[0:32, :]
    om_ref[32:64, :] = bm_ref[32:64, :] + rm_ref[64:96, :]


def ring_end_kernel(own_ref, rp_ref, rm_ref, k_ref, c_ref, z_ref):
    for at, ref in ((0, k_ref), (16, c_ref), (32, z_ref)):
        rows = slice(at, at + ref.shape[0])
        ref[...] = own_ref[rows, :] + rp_ref[rows, :] + rm_ref[rows, :]


def ring_end_last_kernel(own_ref, rp_ref, rm_ref, before_ref, got_ref, k_ref, c_ref, z_ref, zc_ref):
    width = k_ref.shape[1]
    c_ref[:, 0 : before_ref.shape[1]] = before_ref[...] + got_ref[16:32, :]
    for i, ref in enumerate((k_ref, c_ref.at[:, c_ref.shape[1] - width :], z_ref, zc_ref)):
        rows = slice(i * 16, (i + 1) * 16)
        ref[...] = own_ref[rows, :] + rp_ref[rows, :] + rm_ref[rows, :]


def protos_kernel(core_ref, k0_ref, z0_ref, k1_ref, z1_ref, x1_ref, c_ref, out_ref):
    half = out_ref.shape[1] // 2
    at = k0_ref.shape[1]
    mine = core_ref[0] * half
    theirs = (1 - core_ref[0]) * half
    columns = lambda start, width: pl.ds(pl.multiple_of(start, 128), width)
    out_ref[:, columns(mine, at)] = k0_ref[...] + z0_ref[0:16, :]
    out_ref[:, columns(theirs, at)] = c_ref[:, 0:at]
    out_ref[:, columns(mine + at, half - at)] = k1_ref[...] + z1_ref[...]
    out_ref[:, columns(theirs + at, half - at)] = c_ref[:, at:half] + x1_ref[...]


def sum4_kernel(a_ref, b_ref, c_ref, d_ref, out_ref):
    out_ref[...] = a_ref[...] + b_ref[...] + c_ref[...] + d_ref[...]


def add2_kernel(a_ref, b_ref, out_ref):
    out_ref[...] = a_ref[...] + b_ref[...]


def rows_kernel(x_ref, a_ref, b_ref, rows_ref, out_ref):
    total = a_ref[...] + b_ref[...]
    v = rows_ref[...].astype(F32)
    norm = jnp.sqrt(jnp.sum(v * v, axis=1, keepdims=True) + norm_eps)
    z = v / norm
    out_ref[...] = (total - z * jnp.sum(z * total, axis=1, keepdims=True)) / norm


def place_kernel(x_ref, a_ref, p_ref, m_ref, t_ref, out_ref):
    size = a_ref.shape[0]
    for step, ref in ((0, a_ref), (3, p_ref), (1, m_ref), (2, t_ref)):
        rows = pl.ds(pl.multiple_of(lax.rem(x_ref[0] + step, 4) * size, 16), size)
        out_ref[rows, :] = ref[...]


def dp_pairs(move):
    def at(z, y, c):
        return (z * 4 + y) * 2 + c
    return [(at(z, y, c), at(*move(z, y, c))) for z in range(2) for y in range(4) for c in range(2)]


def mp_pairs(dx, dz):
    return [(x * 4 + z, (x + dx) % 4 * 4 + (z + dz) % 4) for x in range(4) for z in range(4)]


CORE = dp_pairs(lambda z, y, c: (z, y, 1 - c))
YP = dp_pairs(lambda z, y, c: (z, (y + 1) % 4, c))
YM = dp_pairs(lambda z, y, c: (z, (y - 1) % 4, c))
ZZ = dp_pairs(lambda z, y, c: (1 - z, y, c))
ZZC = dp_pairs(lambda z, y, c: (1 - z, y, 1 - c))


def to_dp(v, pairs):
    return lax.ppermute(v, "dp", pairs)


def swap_z(v, bit):
    return lax.ppermute(v, "mp", [(i, i ^ bit) for i in range(16)])


def to_mp(v, dx, dz):
    return lax.ppermute(v, "mp", mp_pairs(dx, dz))


VM = pl.BlockSpec(memory_space=pltpu.VMEM)
SM = pl.BlockSpec(memory_space=pltpu.SMEM)


def local(student_rows, teacher_rows, student_protos, teacher_protos, center, row_weight):
    rows, feats = student_rows.shape
    protos = student_protos.shape[1]
    half = protos // 2
    dp = lax.axis_index("dp")
    core, y, z_hi = dp % 2, dp // 2 % 4, dp // 8
    x = lax.axis_index("mp") // 4
    core_s = core.astype(jnp.int32)[None]
    x_s = x.astype(jnp.int32)[None]
    blocks = jnp.stack([
        ((z_hi ^ zr) * 4 + (y + yr) % 4) * 2 + (core ^ cr)
        for yr in (0, 1, 3, 2) for zr in (0, 1) for cr in (0, 1)
    ]).astype(jnp.int32)
    source = jnp.repeat(blocks, 16) * 16 + jnp.arange(feats, dtype=jnp.int32) % 16
    perm = (source[:, None] == jnp.arange(feats, dtype=jnp.int32)[None, :]).astype(BF16)
    hbm = lambda v: pltpu.with_memory_space_constraint(v, pltpu.HBM)

    row_tile = pl.BlockSpec((rows // 2, feats), lambda i: (i, 0))
    z = call(prep_kernel, shape((2, rows, feats)), hbm(student_rows), hbm(teacher_rows), grid=(2,),
             in_specs=[row_tile, row_tile], out_specs=VM, nbytes=3 * MIB)
    z_other = to_dp(z, CORE)

    tiles = half // TILE
    center2 = center[None, :]
    weight2 = row_weight[None, :]
    wide = lambda i, c: (0, c[0] * tiles + i)
    w_wide = pl.BlockSpec((feats, TILE), wide)
    e_shape = pltpu.VMEM((rows, half), BF16)
    w_shape = shape((feats, half), BF16)
    pass_scratch = (pltpu.VMEM((2, rows, feats), BF16), pltpu.VMEM((2, rows, 128), F32))
    flops = 4 * rows * feats * half
    es_o, et_o, ws, wt, inv, sums = call(
        functools.partial(own_kernel, tiles - 1),
        (e_shape, e_shape, w_shape, w_shape, shape((1, half)), shape((2, rows))),
        core_s, z, hbm(student_protos), hbm(teacher_protos), center2,
        scalars=1, grid=(tiles,), in_specs=[VM, w_wide, w_wide, pl.BlockSpec((1, TILE), wide)],
        out_specs=[VM] * 6, scratch_shapes=pass_scratch,
        vmem=14, flops=flops, nbytes=8 * MIB,
    )
    es_x, et_x, pay = call(
        functools.partial(other_kernel, tiles - 1),
        (e_shape, e_shape, shape((8, rows))),
        core_s, z_other, ws, wt, center2, sums, weight2,
        scalars=1, grid=(tiles,), in_specs=[VM, VM, VM, pl.BlockSpec((1, TILE), wide), VM, VM],
        out_specs=[VM] * 3, scratch_shapes=pass_scratch,
        vmem=14, flops=flops, nbytes=8 * MIB,
    )
    small = dict(in_specs=[VM] * 2, out_specs=VM)
    small4 = dict(in_specs=[VM] * 4, out_specs=VM)

    tot1 = call(chip_kernel, shape((8, rows)), pay, to_dp(pay, CORE), **small)
    tot2 = call(add4_kernel, shape((8, rows)), tot1, *[to_mp(tot1, k, 0) for k in (1, 2, 3)], **small4)
    tot = [tot2] + [to_mp(tot2, 0, k) for k in (1, 2, 3)]

    def unit(es, et, zz, after):
        return call(
            unit_kernel, (shape((2, rows, feats)), shape((feats, rows), BF16)), es, et, ws, zz, perm,
            in_specs=[VM] * 5, out_specs=[VM] * 2, after=after, vmem=16, flops=flops, nbytes=8 * MIB,
        )

    u_x, zt_x = unit(es_x, et_x, z_other, (tot1,))
    u_o, zt_o = unit(es_o, et_o, z, (tot2,))
    fac = [pltpu.VMEM((2, rows, 128), F32)]
    zs, f, mixed = call(scale_kernel, (shape((feats, 4 * rows), BF16), shape((4, rows)), shape((rows, feats))), *tot, zt_o, zt_x, u_x,
                        in_specs=[VM] * 7, out_specs=[VM] * 3, scratch_shapes=fac)
    got = to_dp(mixed, CORE)

    def chunk(at, width, after):
        first = at // PART
        own = lambda i, b: (0, i)
        col = lambda i, b: (0, first + i)
        e_tile = pl.BlockSpec((rows, PART), col)
        return call(
            grad_kernel, (*[shape((64, width))] * 3, *[shape((32, width))] * 2),
            blocks, zs, hbm(es_o), hbm(et_o), hbm(es_x), hbm(et_x), ws, inv,
            scalars=1, grid=(width // PART,),
            in_specs=[VM] + [e_tile] * 4 + [pl.BlockSpec((feats, PART), col), pl.BlockSpec((1, PART), col)],
            out_specs=[pl.BlockSpec((64, PART), own)] * 3 + [pl.BlockSpec((32, PART), own)] * 2,
            after=after, vmem=24, flops=2 * flops * width // half, nbytes=26 * MIB * width // half,
        )

    quarter = shape((rows // 4, feats))
    w0, w1 = CHUNKS
    own0, bp0, bm0, ap0, am0 = chunk(0, w0, ())
    o0, op, om, o2 = call(combine_kernel, (quarter,) * 4, x_s, f, u_o, got, after=(ap0,),
                          in_specs=[SM, VM, VM, VM], out_specs=[VM] * 4, scratch_shapes=fac)
    own1, bp1, bm1, ap1, am1 = chunk(w0, w1, (o0,))
    part = call(sum4_kernel, quarter, o0, to_mp(op, 1, 0), to_mp(om, 3, 0), to_mp(o2, 2, 0), **small4)
    mp, mm = call(ring_kernel, (shape((96, w0)),) * 2, bp0, bm0, ap1, am1, to_dp(ap0, YP), to_dp(am0, YM),
                  after=(part,), in_specs=[VM] * 6, out_specs=[VM] * 2)
    gp, gm = to_dp(mp, YP), to_dp(mm, YM)
    pair = call(add2_kernel, quarter, part, swap_z(part, 1), **small)
    fixed = pl.BlockSpec((rows // 4, feats), lambda i, c: (0, 0))
    mine = call(rows_kernel, quarter, x_s, pair, swap_z(pair, 2), hbm(student_rows),
                scalars=1, grid=(1,), in_specs=[fixed] * 2 + [pl.BlockSpec((rows // 4, feats), lambda i, c: (c[0], 0))],
                out_specs=fixed)
    bp1, bm1 = call(ring_last_kernel, (shape((64, w1)),) * 2, bp1, bm1, gp, gm, after=(mine,),
                    in_specs=[VM] * 4, out_specs=[VM] * 2)
    keep0, c0, zz0 = call(ring_end_kernel, (shape((16, w0)), shape((16, w0)), shape((32, w0))), own0, gp, gm,
                          after=(bp1,), in_specs=[VM] * 3, out_specs=[VM] * 3)
    got0 = to_dp(zz0, ZZ)
    keep1, c1, zz1, zc1 = call(
        ring_end_last_kernel, (shape((16, w1)), shape((16, half)), shape((16, w1)), shape((16, w1))),
        own1, to_dp(bp1, YP), to_dp(bm1, YM), c0, got0, in_specs=[VM] * 5, out_specs=[VM] * 4)
    parts = [keep0, got0, keep1, to_dp(zz1, ZZ), to_dp(zc1, ZZC), to_dp(c1, CORE)]
    grad_rows = call(place_kernel, shape((rows, feats)), x_s, mine, to_mp(mine, 1, 0), to_mp(mine, 3, 0), to_mp(mine, 2, 0),
                     in_specs=[SM] + [VM] * 4, out_specs=VM)
    proto_grad = call(protos_kernel, shape((16, protos)), core_s, *parts,
                      in_specs=[SM] + [VM] * len(parts), out_specs=VM)
    return grad_rows, proto_grad


def solution(mesh):
    placed = (P("dp", None), P("dp", None), P(None, "mp"), P(None, "mp"), P("mp"), P("dp"))
    return jax.shard_map(
        local, mesh=mesh, in_specs=placed, out_specs=(P("dp", None), P("dp", "mp")), check_vma=False
    )
```
